32 devices in a mesh: rep: 2 (over y), seq: 4 (over x, core), head: 4 (over z).
Axes of the slice: x: 2, y: 2, z: 4, core: 2. Of those that a mesh axis runs over, the one named last changes fastest.
Arguments:
- queries: bfloat16 [2048, 4096], P(('rep', 'seq', 'head')), parts along dimension 0, may hold values from -6 to 6
- key_rows: bfloat16 [2048, 4096], P(('rep', 'seq', 'head')), parts along dimension 0, may hold values from -6 to 6
- value_rows: bfloat16 [2048, 4096], P(('rep', 'seq', 'head')), parts along dimension 0, may hold values from -6 to 6
- out_grad: bfloat16 [2048, 4096], P(('rep', 'seq', 'head')), parts along dimension 0, may hold values from -6 to 6
Outputs:
- attended: bfloat16 [2048, 4096], P(('rep', 'seq', 'head')), parts along dimension 0
- query_grad: bfloat16 [2048, 4096], P(('rep', 'seq', 'head')), parts along dimension 0
- key_grad: bfloat16 [2048, 4096], P(('rep', 'seq', 'head')), parts along dimension 0
- value_grad: bfloat16 [2048, 4096], P(('rep', 'seq', 'head')), parts along dimension 0
The draws below stay inside these ranges and needn't reach their ends.
There are 2 independent parts, one for each index of `rep`. The reference program is written for one: setup_inputs(seed, part) draws one part's arguments, and reference() takes and returns one part's arrays. A program takes and returns all parts, laid end to end along the dimension named above; each array names one. Nothing has to cross between parts.
All inputs are finite; a program needn't handle non-finite values.
Results may differ from the reference program's by a relative error of at most 0.0049.
Values may be sent and summed in bfloat16 or wider, within the bound.
A program may use at most 64 MiB of HBM per device.

```python
import jax
import jax.numpy as jnp
from jax import lax

H = 32
DH = 128
SEQ = 1024
BLOCK = 256


def steps_of(own_key, extent, shards, low, largest):
    def one(axis_at, blocks):
        steps = jax.random.uniform(jax.random.fold_in(jax.random.fold_in(own_key, 6), axis_at), (blocks,), jnp.float32, low / len(shards), largest / len(shards))
        return jnp.repeat(jnp.exp(steps), extent[axis_at] // blocks).reshape((-1,) + (1,) * (len(extent) - axis_at - 1))

    factor_of = one(*shards[0])
    for cut in shards[1:]:
        factor_of = factor_of * one(*cut)
    return factor_of


def normal_values(rng, extent, width, limit, cuts=(), held_as=jnp.bfloat16):
    values = width * jax.random.normal(rng, extent, jnp.float32)
    if cuts:
        values = values * steps_of(rng, extent, cuts, -0.22, 0.18)
    return jnp.clip(values, -limit, limit).astype(held_as)


def setup_inputs(seed: int = 0, part: int = 0) -> dict:
    splits = jax.random.split(jax.random.key(seed), 5)
    part_splits = jax.random.split(jax.random.fold_in(splits[4], part), 5)
    return {
        "queries": normal_values(part_splits[0], (SEQ, H * DH), 1.0, 6.0, ((0, 16),)),
        "key_rows": normal_values(part_splits[1], (SEQ, H * DH), 1.0, 6.0, ((0, 16),)),
        "value_rows": normal_values(part_splits[2], (SEQ, H * DH), 1.0, 6.0, ((0, 16),)),
        "out_grad": normal_values(part_splits[3], (SEQ, H * DH), 1.0, 6.0, ((0, 16),)),
    }


def head_pass(operands):
    query_part, key_part, value_part, grad_part = operands
    f32 = jnp.float32
    factor = float(DH * SEQ) ** -0.5
    block_count = SEQ // BLOCK
    query_blocks = query_part.reshape(block_count, BLOCK, DH).astype(f32)
    key_blocks = key_part.reshape(block_count, BLOCK, DH).astype(f32)
    value_blocks = value_part.reshape(block_count, BLOCK, DH).astype(f32)
    grad_blocks = grad_part.reshape(block_count, BLOCK, DH).astype(f32)
    kv_state = jnp.einsum("btd,bte->bde", key_blocks, value_blocks)
    grad_state = jnp.einsum("btd,bte->bde", query_blocks, grad_blocks)
    empty_state = jnp.zeros((1, DH, DH), f32)
    prefix = jnp.concatenate([empty_state, jnp.cumsum(kv_state, 0)[:-1]], 0)
    tail_sums = jnp.cumsum(grad_state[::-1], 0)[::-1]
    suffix = jnp.concatenate([tail_sums[1:], empty_state], 0)
    prefix = prefix.astype(jnp.bfloat16).astype(f32)
    suffix = suffix.astype(jnp.bfloat16).astype(f32)
    causal = jnp.arange(BLOCK)[:, None] >= jnp.arange(BLOCK)[None, :]
    scores = jnp.where(causal[None], jnp.einsum("btd,bsd->bts", query_blocks, key_blocks) * factor, 0.0)
    scores = scores.astype(jnp.bfloat16).astype(f32)
    attended = jnp.einsum("bts,bsd->btd", scores, value_blocks) + factor * jnp.einsum("btd,bde->bte", query_blocks, prefix)
    dscores = jnp.where(causal[None], jnp.einsum("bte,bse->bts", grad_blocks, value_blocks) * factor, 0.0)
    dscores = dscores.astype(jnp.bfloat16).astype(f32)
    query_grad = jnp.einsum("bts,bsd->btd", dscores, key_blocks) + factor * jnp.einsum("bte,bde->btd", grad_blocks, prefix)
    key_grad = jnp.einsum("bts,btd->bsd", dscores, query_blocks) + factor * jnp.einsum("bse,bde->bsd", value_blocks, suffix)
    value_grad = jnp.einsum("bts,bte->bse", scores, grad_blocks) + factor * jnp.einsum("bsd,bde->bse", key_blocks, suffix)
    return tuple(item.reshape(SEQ, DH).astype(jnp.bfloat16) for item in (attended, query_grad, key_grad, value_grad))


def to_heads(matrix):
    return matrix.reshape(SEQ, H, DH).transpose(1, 0, 2)


def from_heads(stacked):
    return stacked.transpose(1, 0, 2).reshape(SEQ, H * DH)


def reference(queries, key_rows, value_rows, out_grad):
    results = lax.map(head_pass, (to_heads(queries), to_heads(key_rows), to_heads(value_rows), to_heads(out_grad)))
    return (from_heads(results[0]), from_heads(results[1]), from_heads(results[2]), from_heads(results[3]))
```

```python
import functools

import jax
import jax.numpy as jnp
from jax import lax
from jax.experimental import pallas as pl
from jax.experimental.pallas import tpu as pltpu
from jax.sharding import PartitionSpec as P

DH = 128
HEADS_PER_CHUNK = 2
SEQ_LAG = 1
TOK_LAG = 1

F32 = jnp.float32
BF16 = jnp.bfloat16


def dot(a, b, ca, cb):
    return lax.dot_general(a, b, (((ca,), (cb,)), ((), ())), preferred_element_type=F32)


def kernel(
    n_s, n_h, heads, per, factor, zdt,
    q_ref, k_ref, v_ref, g_ref,
    att_ref, dq_ref, dk_ref, dv_ref,
    own_kv, own_gs, s_send, s_recv, t_send, t_recv,
    up_send, up_recv, dn_send, dn_recv,
    s_ss, s_rs, t_ss, t_rs, up_ss, up_rs, dn_ss, dn_rs,
):
    s = lax.axis_index("seq")
    h = lax.axis_index("head")
    chunks = heads // per
    toks = q_ref.shape[0]

    def seq_copy(src, dst, ss, rs, i, to):
        return pltpu.make_async_remote_copy(
            src_ref=src.at[pl.ds(i * per, per)],
            dst_ref=dst.at[pl.ds(i * per, per)],
            send_sem=ss.at[i],
            recv_sem=rs.at[i],
            device_id={"seq": to},
            device_id_type=pl.DeviceIdType.MESH,
        )

    def head_copy(src, dst, ss, rs, i, to):
        return pltpu.make_async_remote_copy(
            src_ref=src.at[i],
            dst_ref=dst.at[i],
            send_sem=ss.at[i],
            recv_sem=rs.at[i],
            device_id={"head": to},
            device_id_type=pl.DeviceIdType.MESH,
        )

    s_next, s_prev = lax.rem(s + 1, n_s), lax.rem(s + n_s - 1, n_s)
    h_next, h_prev = lax.rem(h + 1, n_h), lax.rem(h + n_h - 1, n_h)

    def fwd(i):
        return seq_copy(s_send, s_recv, s_ss, s_rs, i, s_next)

    def bwd(i):
        return seq_copy(t_send, t_recv, t_ss, t_rs, i, s_prev)

    def up(i):
        return head_copy(up_send, up_recv, up_ss, up_rs, i, h_next)

    def down(i):
        return head_copy(dn_send, dn_recv, dn_ss, dn_rs, i, h_prev)

    s_first, s_last = s == 0, s == n_s - 1
    h_first, h_last = h == 0, h == n_h - 1

    barrier = pltpu.get_barrier_semaphore()

    def greet(cond, **to):
        @pl.when(cond)
        def _():
            pl.semaphore_signal(barrier, inc=1, device_id=to, device_id_type=pl.DeviceIdType.MESH)

    greet(jnp.logical_not(s_first), seq=s_prev)
    greet(jnp.logical_not(s_last), seq=s_next)
    greet(jnp.logical_not(h_first), head=h_prev)
    greet(jnp.logical_not(h_last), head=h_next)

    @pl.when(s_first)
    def _():
        s_recv[...] = jnp.zeros_like(s_recv)

    @pl.when(s_last)
    def _():
        t_recv[...] = jnp.zeros_like(t_recv)

    @pl.when(h_first)
    def _():
        up_recv[...] = jnp.zeros_like(up_recv)

    @pl.when(h_last)
    def _():
        dn_recv[...] = jnp.zeros_like(dn_recv)

    def cols(j):
        return pl.ds(pl.multiple_of(j * DH, DH), DH)

    def states(i):
        for r in range(per):
            j = i * per + r
            own_kv[j] = dot(k_ref[:, cols(j)], v_ref[:, cols(j)], 0, 0)
            own_gs[j] = dot(q_ref[:, cols(j)], g_ref[:, cols(j)], 0, 0)

    row = lax.broadcasted_iota(jnp.int32, (toks, toks), 0)
    col = lax.broadcasted_iota(jnp.int32, (toks, toks), 1)
    causal = row >= col

    def apply(i):
        for r in range(per):
            j = i * per + r
            at = cols(j)
            q, k, v, g = q_ref[:, at], k_ref[:, at], v_ref[:, at], g_ref[:, at]
            prefix = up_recv[i, 0, r].astype(F32) + s_recv[j] + dn_recv[i, 0, r].astype(F32)
            suffix = dn_recv[i, 1, r].astype(F32) + t_recv[j] + up_recv[i, 1, r].astype(F32)
            prefix = (prefix * factor).astype(BF16)
            suffix = (suffix * factor).astype(BF16)
            scores = jnp.where(causal, dot(q, k, 1, 1) * factor, 0.0).astype(BF16)
            dscores = jnp.where(causal, dot(g, v, 1, 1) * factor, 0.0).astype(BF16)
            att_ref[:, at] = (dot(scores, v, 1, 0) + dot(q, prefix, 1, 0)).astype(BF16)
            dq_ref[:, at] = (dot(dscores, k, 1, 0) + dot(g, prefix, 1, 1)).astype(BF16)
            dk_ref[:, at] = (dot(dscores, q, 0, 0) + dot(v, suffix, 1, 1)).astype(BF16)
            dv_ref[:, at] = (dot(scores, g, 0, 0) + dot(k, suffix, 1, 0)).astype(BF16)

    states(0)
    pl.semaphore_wait(
        barrier,
        4 - s_first.astype(jnp.int32) - s_last.astype(jnp.int32)
        - h_first.astype(jnp.int32) - h_last.astype(jnp.int32),
    )

    off_c = SEQ_LAG * (n_s - 1)
    off_e = off_c + TOK_LAG * (n_h - 1)

    def valid(i, *more):
        ok = jnp.logical_and(i >= 0, i < chunks)
        for cond in more:
            ok = jnp.logical_and(ok, cond)
        return ok

    def slot(t, carry):
        i = t - SEQ_LAG * s

        @pl.when(valid(i, s > 0))
        def _():
            fwd(i).wait_recv()

        @pl.when(valid(i, s < n_s - 1))
        def _():
            at = pl.ds(i * per, per)
            s_send[at] = s_recv[at] + own_kv[at]
            fwd(i).start()

        b = t - SEQ_LAG * (n_s - 1 - s)

        @pl.when(valid(b, s < n_s - 1))
        def _():
            bwd(b).wait_recv()

        @pl.when(valid(b, s > 0))
        def _():
            at = pl.ds(b * per, per)
            t_send[at] = t_recv[at] + own_gs[at]
            bwd(b).start()

        u = t - off_c - TOK_LAG * h

        @pl.when(valid(u, h > 0))
        def _():
            up(u).wait_recv()

        @pl.when(valid(u, h < n_h - 1))
        def _():
            at = pl.ds(u * per, per)
            up_send[u, 0] = (up_recv[u, 0].astype(F32) + (s_recv[at] + own_kv[at])).astype(zdt)
            up_send[u, 1] = (up_recv[u, 1].astype(F32) + t_recv[at]).astype(zdt)
            up(u).start()

        d = t - off_c - TOK_LAG * (n_h - 1 - h)

        @pl.when(valid(d, h < n_h - 1))
        def _():
            down(d).wait_recv()

        @pl.when(valid(d, h > 0))
        def _():
            at = pl.ds(d * per, per)
            dn_send[d, 1] = (dn_recv[d, 1].astype(F32) + (t_recv[at] + own_gs[at])).astype(zdt)
            dn_send[d, 0] = (dn_recv[d, 0].astype(F32) + s_recv[at]).astype(zdt)
            down(d).start()

        @pl.when(t + 1 < chunks)
        def _():
            states(t + 1)

        e = t - off_e

        @pl.when(valid(e))
        def _():
            apply(e)

        return carry

    lax.fori_loop(0, chunks + off_e, slot, 0)

    def drain(i, carry):
        @pl.when(s < n_s - 1)
        def _():
            fwd(i).wait_send()

        @pl.when(s > 0)
        def _():
            bwd(i).wait_send()

        @pl.when(h < n_h - 1)
        def _():
            up(i).wait_send()

        @pl.when(h > 0)
        def _():
            down(i).wait_send()

        return carry

    lax.fori_loop(0, chunks, drain, 0)


def solution(mesh):
    n_s, n_h = mesh.shape["seq"], mesh.shape["head"]

    def shards(queries, key_rows, value_rows, out_grad):
        toks, width = queries.shape
        heads = width // DH
        per = HEADS_PER_CHUNK
        chunks = heads // per
        factor = float(DH * toks * n_h * n_s) ** (-0.5)
        zdt = BF16 if n_h <= 4 else F32
        state = pltpu.VMEM((heads, DH, DH), F32)
        hop = pltpu.VMEM((chunks, 2, per, DH, DH), zdt)
        vmem = pl.BlockSpec(memory_space=pltpu.VMEM)
        return pl.pallas_call(
            functools.partial(kernel, n_s, n_h, heads, per, factor, zdt),
            out_shape=[jax.ShapeDtypeStruct((toks, width), BF16)] * 4,
            in_specs=[vmem] * 4,
            out_specs=[vmem] * 4,
            scratch_shapes=[state] * 6 + [hop] * 4 + [pltpu.SemaphoreType.DMA((chunks,))] * 8,
            compiler_params=pltpu.CompilerParams(
                collective_id=0, has_side_effects=True, vmem_limit_bytes=48 * 1024 * 1024
            ),
        )(queries, key_rows, value_rows, out_grad)

    placed = (P(("rep", "seq", "head"), None),) * 4
    return jax.shard_map(
        shards, mesh=mesh, in_specs=placed, out_specs=placed, check_vma=False
    )
```

```python
import functools

import jax
import jax.numpy as jnp
from jax import lax
from jax.experimental import pallas as pl
from jax.experimental.pallas import tpu as pltpu
from jax.sharding import PartitionSpec as P

DH = 128
SPLIT = 1
CORE_LAG = 1
CHIP_LAG = 2
TOK_LAG = 3
GROUP = 8
VMEM = 62 * 1024 * 1024

F32 = jnp.float32
BF16 = jnp.bfloat16
MESH = pl.DeviceIdType.MESH


def dot(a, b, ca, cb):
    return lax.dot_general(a, b, (((ca,), (cb,)), ((), ())), preferred_element_type=F32)


def kernel(
    n_s, n_h, heads, factor, xdt, zdt,
    q_hbm, k_hbm, v_hbm, g_hbm,
    att_hbm, dq_hbm, dk_hbm, dv_hbm,
    q_ref, k_ref, v_ref, g_ref, att_ref, dq_ref, dk_ref, dv_ref,
    own, pair, s_all, t_all, f_send, f_recv, b_send, b_recv,
    up_send, up_recv, dn_send, dn_recv,
    in_sem, out_sem, c_ss, c_rs, f_ss, f_rs, b_ss, b_rs, up_ss, up_rs, dn_ss, dn_rs,
):
    s = lax.axis_index("seq")
    h = lax.axis_index("head")
    n_p = n_s // 2
    p, c = s // 2, lax.rem(s, 2)
    units = heads * SPLIT
    rows = DH // SPLIT
    toks = q_ref.shape[0]
    groups = heads // GROUP

    def fetch(g):
        at = pl.ds(pl.multiple_of(g * GROUP * DH, GROUP * DH), GROUP * DH)
        return [
            pltpu.make_async_copy(src.at[:, at], dst.at[:, at], in_sem.at[n, g])
            for n, (src, dst) in enumerate(
                ((k_hbm, k_ref), (v_hbm, v_ref), (q_hbm, q_ref), (g_hbm, g_ref))
            )
        ]

    def put(g):
        at = pl.ds(pl.multiple_of(g * GROUP * DH, GROUP * DH), GROUP * DH)
        return [
            pltpu.make_async_copy(src.at[:, at], dst.at[:, at], out_sem.at[n, g])
            for n, (src, dst) in enumerate(
                ((att_ref, att_hbm), (dq_ref, dq_hbm), (dk_ref, dk_hbm), (dv_ref, dv_hbm))
            )
        ]

    for g in range(groups):
        for copy in fetch(g):
            copy.start()

    def remote(src, dst, ss, rs, i, to):
        return pltpu.make_async_remote_copy(
            src_ref=src, dst_ref=dst, send_sem=ss.at[i], recv_sem=rs.at[i],
            device_id=to, device_id_type=MESH,
        )

    other = 2 * p + (1 - c)
    s_up, s_dn = lax.rem(s + 2, n_s), lax.rem(s + n_s - 2, n_s)
    h_up, h_dn = lax.rem(h + 1, n_h), lax.rem(h + n_h - 1, n_h)

    def swap(i):
        return remote(own.at[i], pair.at[i], c_ss, c_rs, i, {"seq": other})

    def fwd(i):
        return remote(f_send.at[i], f_recv.at[i], f_ss, f_rs, i, {"seq": s_up})

    def bwd(i):
        return remote(b_send.at[i], b_recv.at[i], b_ss, b_rs, i, {"seq": s_dn})

    def up(i, n):
        return remote(
            up_send.at[i, pl.ds(0, n)], up_recv.at[i, pl.ds(0, n)], up_ss, up_rs, i, {"head": h_up}
        )

    def down(i, n):
        return remote(
            dn_send.at[i, pl.ds(0, n)], dn_recv.at[i, pl.ds(0, n)], dn_ss, dn_rs, i, {"head": h_dn}
        )

    p_first, p_last = p == 0, p == n_p - 1
    s_first, s_last = s == 0, s == n_s - 1
    h_first, h_last = h == 0, h == n_h - 1
    no = jnp.logical_not

    barrier = pltpu.get_barrier_semaphore()

    def greet(**to):
        pl.semaphore_signal(barrier, inc=1, device_id=to, device_id_type=MESH)

    greet(seq=other)
    pl.when(no(p_first))(lambda: greet(seq=s_dn))
    pl.when(no(p_last))(lambda: greet(seq=s_up))
    pl.when(no(h_first))(lambda: greet(head=h_dn))
    pl.when(no(h_last))(lambda: greet(head=h_up))

    @pl.when(p_first)
    def _():
        f_recv[...] = jnp.zeros_like(f_recv)

    @pl.when(p_last)
    def _():
        b_recv[...] = jnp.zeros_like(b_recv)

    @pl.when(h_first)
    def _():
        up_recv[:, 0] = jnp.zeros_like(up_recv[:, 0])

    @pl.when(h_last)
    def _():
        dn_recv[:, 0] = jnp.zeros_like(dn_recv[:, 0])

    @pl.when(jnp.logical_or(h_first, s_last))
    def _():
        up_recv[:, 1] = jnp.zeros_like(up_recv[:, 1])

    @pl.when(jnp.logical_or(h_last, s_first))
    def _():
        dn_recv[:, 1] = jnp.zeros_like(dn_recv[:, 1])

    def cols(j):
        return pl.ds(pl.multiple_of(j * DH, DH), DH)

    def states(j):
        at = cols(j)
        kv = dot(k_ref[:, at], v_ref[:, at], 0, 0)
        gs = dot(q_ref[:, at], g_ref[:, at], 0, 0)
        for r in range(SPLIT):
            own[j * SPLIT + r, 0] = kv[r * rows:(r + 1) * rows]
            own[j * SPLIT + r, 1] = gs[r * rows:(r + 1) * rows]

    row = lax.broadcasted_iota(jnp.int32, (toks, toks), 0)
    col = lax.broadcasted_iota(jnp.int32, (toks, toks), 1)
    causal = row >= col

    def apply(j):
        at = cols(j)
        q, k, v, g = q_ref[:, at], k_ref[:, at], v_ref[:, at], g_ref[:, at]
        part = pl.ds(j * SPLIT, SPLIT)
        prefix = up_recv[part, 0].astype(F32) + s_all[part] + dn_recv[part, 1].astype(F32)
        suffix = dn_recv[part, 0].astype(F32) + t_all[part] + up_recv[part, 1].astype(F32)
        prefix = (prefix * factor).astype(BF16).reshape(DH, DH)
        suffix = (suffix * factor).astype(BF16).reshape(DH, DH)
        scores = jnp.where(causal, dot(q, k, 1, 1) * factor, 0.0).astype(BF16)
        dscores = jnp.where(causal, dot(g, v, 1, 1) * factor, 0.0).astype(BF16)
        att_ref[:, at] = (dot(scores, v, 1, 0) + dot(q, prefix, 1, 0)).astype(BF16)
        dq_ref[:, at] = (dot(dscores, k, 1, 0) + dot(g, prefix, 1, 1)).astype(BF16)
        dk_ref[:, at] = (dot(dscores, q, 0, 0) + dot(v, suffix, 1, 1)).astype(BF16)
        dv_ref[:, at] = (dot(scores, g, 0, 0) + dot(k, suffix, 1, 0)).astype(BF16)

    for copy in fetch(0):
        copy.wait()
    states(0)
    pl.semaphore_wait(
        barrier,
        5 - p_first.astype(jnp.int32) - p_last.astype(jnp.int32)
        - h_first.astype(jnp.int32) - h_last.astype(jnp.int32),
    )
    for r in range(SPLIT):
        swap(r).start()

    off_z = CORE_LAG + CHIP_LAG * (n_p - 1)
    off_e = off_z + TOK_LAG * (n_h - 1)

    def valid(i, *more):
        ok = jnp.logical_and(i >= 0, i < units)
        for cond in more:
            ok = jnp.logical_and(ok, cond)
        return ok

    def slot(t, carry):
        w = t - CORE_LAG

        @pl.when(valid(w))
        def _():
            swap(w).wait_recv()

        f = t - CORE_LAG - CHIP_LAG * p

        @pl.when(valid(f, no(p_first)))
        def _():
            fwd(f).wait_recv()

        @pl.when(valid(f, no(p_last)))
        def _():
            f_send[f] = (f_recv[f].astype(F32) + (own[f, 0] + pair[f, 0])).astype(xdt)
            fwd(f).start()

        b = t - CORE_LAG - CHIP_LAG * (n_p - 1 - p)

        @pl.when(valid(b, no(p_last)))
        def _():
            bwd(b).wait_recv()

        @pl.when(valid(b, no(p_first)))
        def _():
            b_send[b] = (b_recv[b].astype(F32) + (own[b, 1] + pair[b, 1])).astype(xdt)
            bwd(b).start()

        z = t - off_z

        @pl.when(valid(z))
        def _():
            s_all[z] = f_recv[z].astype(F32) + jnp.where(c == 1, pair[z, 0], 0.0)
            t_all[z] = b_recv[z].astype(F32) + jnp.where(c == 0, pair[z, 1], 0.0)

        u = z - TOK_LAG * h

        @pl.when(valid(u, no(h_first), no(s_last)))
        def _():
            up(u, 2).wait_recv()

        @pl.when(valid(u, no(h_first), s_last))
        def _():
            up(u, 1).wait_recv()

        @pl.when(valid(u, no(h_last)))
        def _():
            up_send[u, 0] = (up_recv[u, 0].astype(F32) + (s_all[u] + own[u, 0])).astype(zdt)

            @pl.when(no(s_last))
            def _():
                up_send[u, 1] = (up_recv[u, 1].astype(F32) + t_all[u]).astype(zdt)
                up(u, 2).start()

            @pl.when(s_last)
            def _():
                up(u, 1).start()

        d = z - TOK_LAG * (n_h - 1 - h)

        @pl.when(valid(d, no(h_last), no(s_first)))
        def _():
            down(d, 2).wait_recv()

        @pl.when(valid(d, no(h_last), s_first))
        def _():
            down(d, 1).wait_recv()

        @pl.when(valid(d, no(h_first)))
        def _():
            dn_send[d, 0] = (dn_recv[d, 0].astype(F32) + (t_all[d] + own[d, 1])).astype(zdt)

            @pl.when(no(s_first))
            def _():
                dn_send[d, 1] = (dn_recv[d, 1].astype(F32) + s_all[d]).astype(zdt)
                down(d, 2).start()

            @pl.when(s_first)
            def _():
                down(d, 1).start()

        j = (t + 1) // SPLIT

        @pl.when(jnp.logical_and(lax.rem(t + 1, SPLIT) == 0, j < heads))
        def _():
            @pl.when(lax.rem(j, GROUP) == 0)
            def _():
                for copy in fetch(j // GROUP):
                    copy.wait()

            states(j)
            for r in range(SPLIT):
                swap(j * SPLIT + r).start()

        e = t - off_e

        @pl.when(valid(e, lax.rem(e + 1, SPLIT) == 0))
        def _():
            apply(e // SPLIT)

            @pl.when(lax.rem(e // SPLIT + 1, GROUP) == 0)
            def _():
                for copy in put(e // SPLIT // GROUP):
                    copy.start()

        return carry

    lax.fori_loop(0, units + off_e, slot, 0)

    def drain(i, carry):
        swap(i).wait_send()
        pl.when(no(p_last))(lambda: fwd(i).wait_send())
        pl.when(no(p_first))(lambda: bwd(i).wait_send())
        pl.when(jnp.logical_and(no(h_last), no(s_last)))(lambda: up(i, 2).wait_send())
        pl.when(jnp.logical_and(no(h_last), s_last))(lambda: up(i, 1).wait_send())
        pl.when(jnp.logical_and(no(h_first), no(s_first)))(lambda: down(i, 2).wait_send())
        pl.when(jnp.logical_and(no(h_first), s_first))(lambda: down(i, 1).wait_send())
        return carry

    lax.fori_loop(0, units, drain, 0)
    for g in range(groups):
        for copy in put(g):
            copy.wait()


def solution(mesh):
    n_s, n_h = mesh.shape["seq"], mesh.shape["head"]

    def shards(queries, key_rows, value_rows, out_grad):
        toks, width = queries.shape
        heads = width // DH
        units, rows = heads * SPLIT, DH // SPLIT
        factor = float(DH * toks * n_h * n_s) ** (-0.5)
        xdt = BF16 if n_s <= 4 else F32
        zdt = BF16 if n_h <= 4 else F32
        tokens = pltpu.VMEM((toks, width), BF16)
        both = pltpu.VMEM((units, 2, rows, DH), F32)
        one = pltpu.VMEM((units, rows, DH), F32)
        chip = pltpu.VMEM((units, rows, DH), xdt)
        hop = pltpu.VMEM((units, 2, rows, DH), zdt)
        hbm = pl.BlockSpec(memory_space=pltpu.HBM)
        shape = [jax.ShapeDtypeStruct((toks, width), BF16)] * 4
        dma = pltpu.SemaphoreType.DMA
        return pl.pallas_call(
            functools.partial(kernel, n_s, n_h, heads, factor, xdt, zdt),
            out_shape=shape,
            in_specs=[hbm] * 4,
            out_specs=[hbm] * 4,
            scratch_shapes=[tokens] * 8
            + [both] * 2 + [one] * 2 + [chip] * 4 + [hop] * 4
            + [dma((4, heads // GROUP))] * 2 + [dma((units,))] * 10,
            compiler_params=pltpu.CompilerParams(
                collective_id=0, has_side_effects=True, vmem_limit_bytes=VMEM
            ),
        )(queries, key_rows, value_rows, out_grad)

    placed = (P(("rep", "seq", "head"), None),) * 4
    return jax.shard_map(
        shards, mesh=mesh, in_specs=placed, out_specs=placed, check_vma=False
    )
```

```python
import functools

import jax
import jax.numpy as jnp
from jax import lax
from jax.experimental import pallas as pl
from jax.experimental.pallas import tpu as pltpu
from jax.sharding import PartitionSpec as P

DH = 128
SPLIT = 1
CORE_LAG = 1
CHIP_LAG = 2
TOK_LAG = 3
GROUP = 8
STEPS = 2
VMEM = 62 * 1024 * 1024

F32 = jnp.float32
BF16 = jnp.bfloat16
MESH = pl.DeviceIdType.MESH


def dot(a, b, ca, cb):
    return lax.dot_general(a, b, (((ca,), (cb,)), ((), ())), preferred_element_type=F32)


def kernel(
    n_s, n_h, heads, factor, xdt, zdt,
    q_hbm, k_hbm, v_hbm, g_hbm,
    att_hbm, dq_hbm, dk_hbm, dv_hbm,
    q_ref, k_ref, v_ref, g_ref, att_ref, dq_ref, dk_ref, dv_ref,
    own, pair, s_all, t_all, f_send, f_recv, b_send, b_recv,
    up_send, up_recv, dn_send, dn_recv,
    in_sem, out_sem, c_ss, c_rs, f_ss, f_rs, b_ss, b_rs, up_ss, up_rs, dn_ss, dn_rs,
):
    s = lax.axis_index("seq")
    h = lax.axis_index("head")
    n_p = n_s // 2
    p, c = s // 2, lax.rem(s, 2)
    units = heads * SPLIT
    rows = DH // SPLIT
    toks = q_ref.shape[0]
    groups = heads // GROUP

    def fetch(g):
        at = pl.ds(pl.multiple_of(g * GROUP * DH, GROUP * DH), GROUP * DH)
        return [
            pltpu.make_async_copy(src.at[:, at], dst.at[:, at], in_sem.at[n, g])
            for n, (src, dst) in enumerate(
                ((k_hbm, k_ref), (v_hbm, v_ref), (q_hbm, q_ref), (g_hbm, g_ref))
            )
        ]

    def put(g):
        at = pl.ds(pl.multiple_of(g * GROUP * DH, GROUP * DH), GROUP * DH)
        return [
            pltpu.make_async_copy(src.at[:, at], dst.at[:, at], out_sem.at[n, g])
            for n, (src, dst) in enumerate(
                ((att_ref, att_hbm), (dq_ref, dq_hbm), (dk_ref, dk_hbm), (dv_ref, dv_hbm))
            )
        ]

    for g in range(groups):
        for copy in fetch(g):
            copy.start()

    def remote(src, dst, ss, rs, i, to):
        return pltpu.make_async_remote_copy(
            src_ref=src, dst_ref=dst, send_sem=ss.at[i], recv_sem=rs.at[i],
            device_id=to, device_id_type=MESH,
        )

    other = 2 * p + (1 - c)
    s_up, s_dn = lax.rem(s + 2, n_s), lax.rem(s + n_s - 2, n_s)
    h_up, h_dn = lax.rem(h + 1, n_h), lax.rem(h + n_h - 1, n_h)

    def swap(i):
        return remote(own.at[i], pair.at[i], c_ss, c_rs, i, {"seq": other})

    def fwd(i):
        return remote(f_send.at[i], f_recv.at[i], f_ss, f_rs, i, {"seq": s_up})

    def bwd(i):
        return remote(b_send.at[i], b_recv.at[i], b_ss, b_rs, i, {"seq": s_dn})

    def up(i, n):
        return remote(
            up_send.at[i, pl.ds(0, n)], up_recv.at[i, pl.ds(0, n)], up_ss, up_rs, i, {"head": h_up}
        )

    def down(i, n):
        return remote(
            dn_send.at[i, pl.ds(0, n)], dn_recv.at[i, pl.ds(0, n)], dn_ss, dn_rs, i, {"head": h_dn}
        )

    p_first, p_last = p == 0, p == n_p - 1
    s_first, s_last = s == 0, s == n_s - 1
    h_first, h_last = h == 0, h == n_h - 1
    no = jnp.logical_not

    barrier = pltpu.get_barrier_semaphore()

    def greet(**to):
        pl.semaphore_signal(barrier, inc=1, device_id=to, device_id_type=MESH)

    greet(seq=other)
    pl.when(no(p_first))(lambda: greet(seq=s_dn))
    pl.when(no(p_last))(lambda: greet(seq=s_up))
    pl.when(no(h_first))(lambda: greet(head=h_dn))
    pl.when(no(h_last))(lambda: greet(head=h_up))

    @pl.when(p_first)
    def _():
        f_recv[...] = jnp.zeros_like(f_recv)

    @pl.when(p_last)
    def _():
        b_recv[...] = jnp.zeros_like(b_recv)

    @pl.when(h_first)
    def _():
        up_recv[:, 0] = jnp.zeros_like(up_recv[:, 0])

    @pl.when(h_last)
    def _():
        dn_recv[:, 0] = jnp.zeros_like(dn_recv[:, 0])

    @pl.when(jnp.logical_or(h_first, s_last))
    def _():
        up_recv[:, 1] = jnp.zeros_like(up_recv[:, 1])

    @pl.when(jnp.logical_or(h_last, s_first))
    def _():
        dn_recv[:, 1] = jnp.zeros_like(dn_recv[:, 1])

    def cols(j):
        return pl.ds(pl.multiple_of(j * DH, DH), DH)

    def states(j):
        at = cols(j)
        kv = dot(k_ref[:, at], v_ref[:, at], 0, 0)
        gs = dot(q_ref[:, at], g_ref[:, at], 0, 0)
        for r in range(SPLIT):
            own[j * SPLIT + r, 0] = kv[r * rows:(r + 1) * rows]
            own[j * SPLIT + r, 1] = gs[r * rows:(r + 1) * rows]

    row = lax.broadcasted_iota(jnp.int32, (toks, toks), 0)
    col = lax.broadcasted_iota(jnp.int32, (toks, toks), 1)
    causal = row >= col

    def apply(j):
        at = cols(j)
        q, k, v, g = q_ref[:, at], k_ref[:, at], v_ref[:, at], g_ref[:, at]
        part = pl.ds(j * SPLIT, SPLIT)
        prefix = up_recv[part, 0].astype(F32) + s_all[part] + dn_recv[part, 1].astype(F32)
        suffix = dn_recv[part, 0].astype(F32) + t_all[part] + up_recv[part, 1].astype(F32)
        prefix = (prefix * factor).astype(BF16).reshape(DH, DH)
        suffix = (suffix * factor).astype(BF16).reshape(DH, DH)
        scores = jnp.where(causal, dot(q, k, 1, 1) * factor, 0.0).astype(BF16)
        dscores = jnp.where(causal, dot(g, v, 1, 1) * factor, 0.0).astype(BF16)
        att_ref[:, at] = (dot(scores, v, 1, 0) + dot(q, prefix, 1, 0)).astype(BF16)
        dq_ref[:, at] = (dot(dscores, k, 1, 0) + dot(g, prefix, 1, 1)).astype(BF16)
        dk_ref[:, at] = (dot(dscores, q, 0, 0) + dot(v, suffix, 1, 1)).astype(BF16)
        dv_ref[:, at] = (dot(scores, g, 0, 0) + dot(k, suffix, 1, 0)).astype(BF16)

    for copy in fetch(0):
        copy.wait()
    states(0)
    pl.semaphore_wait(
        barrier,
        5 - p_first.astype(jnp.int32) - p_last.astype(jnp.int32)
        - h_first.astype(jnp.int32) - h_last.astype(jnp.int32),
    )
    for r in range(SPLIT):
        swap(r).start()

    off_z = CORE_LAG + CHIP_LAG * (n_p - 1)
    off_e = off_z + TOK_LAG * (n_h - 1)

    def valid(i, *more):
        ok = jnp.logical_and(i >= 0, i < units)
        for cond in more:
            ok = jnp.logical_and(ok, cond)
        return ok

    def slot(t, carry):
        w = t - CORE_LAG

        @pl.when(valid(w))
        def _():
            swap(w).wait_recv()

        f = t - CORE_LAG - CHIP_LAG * p

        @pl.when(valid(f, no(p_first)))
        def _():
            fwd(f).wait_recv()

        @pl.when(valid(f, no(p_last)))
        def _():
            f_send[f] = (f_recv[f].astype(F32) + (own[f, 0] + pair[f, 0])).astype(xdt)
            fwd(f).start()

        b = t - CORE_LAG - CHIP_LAG * (n_p - 1 - p)

        @pl.when(valid(b, no(p_last)))
        def _():
            bwd(b).wait_recv()

        @pl.when(valid(b, no(p_first)))
        def _():
            b_send[b] = (b_recv[b].astype(F32) + (own[b, 1] + pair[b, 1])).astype(xdt)
            bwd(b).start()

        z = t - off_z

        @pl.when(valid(z))
        def _():
            s_all[z] = f_recv[z].astype(F32) + jnp.where(c == 1, pair[z, 0], 0.0)
            t_all[z] = b_recv[z].astype(F32) + jnp.where(c == 0, pair[z, 1], 0.0)

        u = z - TOK_LAG * h

        @pl.when(valid(u, no(h_first), no(s_last)))
        def _():
            up(u, 2).wait_recv()

        @pl.when(valid(u, no(h_first), s_last))
        def _():
            up(u, 1).wait_recv()

        @pl.when(valid(u, no(h_last)))
        def _():
            up_send[u, 0] = (up_recv[u, 0].astype(F32) + (s_all[u] + own[u, 0])).astype(zdt)

            @pl.when(no(s_last))
            def _():
                up_send[u, 1] = (up_recv[u, 1].astype(F32) + t_all[u]).astype(zdt)
                up(u, 2).start()

            @pl.when(s_last)
            def _():
                up(u, 1).start()

        d = z - TOK_LAG * (n_h - 1 - h)

        @pl.when(valid(d, no(h_last), no(s_first)))
        def _():
            down(d, 2).wait_recv()

        @pl.when(valid(d, no(h_last), s_first))
        def _():
            down(d, 1).wait_recv()

        @pl.when(valid(d, no(h_first)))
        def _():
            dn_send[d, 0] = (dn_recv[d, 0].astype(F32) + (t_all[d] + own[d, 1])).astype(zdt)

            @pl.when(no(s_first))
            def _():
                dn_send[d, 1] = (dn_recv[d, 1].astype(F32) + s_all[d]).astype(zdt)
                down(d, 2).start()

            @pl.when(s_first)
            def _():
                down(d, 1).start()

        j = (t + 1) // SPLIT

        @pl.when(jnp.logical_and(lax.rem(t + 1, SPLIT) == 0, j < heads))
        def _():
            @pl.when(lax.rem(j, GROUP) == 0)
            def _():
                for copy in fetch(j // GROUP):
                    copy.wait()

            states(j)
            for r in range(SPLIT):
                swap(j * SPLIT + r).start()

        e = t - off_e

        @pl.when(valid(e, lax.rem(e + 1, SPLIT) == 0))
        def _():
            apply(e // SPLIT)

            @pl.when(lax.rem(e // SPLIT + 1, GROUP) == 0)
            def _():
                for copy in put(e // SPLIT // GROUP):
                    copy.start()

        return carry

    lax.fori_loop(0, units + off_e, slot, 0)

    def drain(i, carry):
        swap(i).wait_send()
        pl.when(no(p_last))(lambda: fwd(i).wait_send())
        pl.when(no(p_first))(lambda: bwd(i).wait_send())
        pl.when(jnp.logical_and(no(h_last), no(s_last)))(lambda: up(i, 2).wait_send())
        pl.when(jnp.logical_and(no(h_last), s_last))(lambda: up(i, 1).wait_send())
        pl.when(jnp.logical_and(no(h_first), no(s_first)))(lambda: down(i, 2).wait_send())
        pl.when(jnp.logical_and(no(h_first), s_first))(lambda: down(i, 1).wait_send())
        return carry

    lax.fori_loop(0, units, drain, 0)
    for g in range(groups):
        for copy in put(g):
            copy.wait()


def store(*refs):
    for src, dst in zip(refs[:4], refs[4:]):
        dst[...] = src[...]


def solution(mesh):
    n_s, n_h = mesh.shape["seq"], mesh.shape["head"]

    def shards(queries, key_rows, value_rows, out_grad):
        toks, width = queries.shape
        heads = width // DH
        units, rows = heads * SPLIT, DH // SPLIT
        factor = float(DH * toks * n_h * n_s) ** (-0.5)
        xdt = BF16 if n_s <= 4 else F32
        zdt = BF16 if n_h <= 4 else F32
        tokens = pltpu.VMEM((toks, width), BF16)
        both = pltpu.VMEM((units, 2, rows, DH), F32)
        one = pltpu.VMEM((units, rows, DH), F32)
        chip = pltpu.VMEM((units, rows, DH), xdt)
        hop = pltpu.VMEM((units, 2, rows, DH), zdt)
        hbm = pl.BlockSpec(memory_space=pltpu.HBM)
        shape = [jax.ShapeDtypeStruct((toks, width), BF16)] * 4
        dma = pltpu.SemaphoreType.DMA
        results = pl.pallas_call(
            functools.partial(kernel, n_s, n_h, heads, factor, xdt, zdt),
            out_shape=shape,
            in_specs=[hbm] * 4,
            out_specs=[hbm] * 4,
            scratch_shapes=[tokens] * 8
            + [both] * 2 + [one] * 2 + [chip] * 4 + [hop] * 4
            + [dma((4, heads // GROUP))] * 2 + [dma((units,))] * 10,
            compiler_params=pltpu.CompilerParams(
                collective_id=0, has_side_effects=True, vmem_limit_bytes=VMEM
            ),
        )(queries, key_rows, value_rows, out_grad)

        block = pl.BlockSpec((toks // STEPS, width), lambda i: (i, 0))
        return pl.pallas_call(
            store,
            grid=(STEPS,),
            out_shape=shape,
            in_specs=[block] * 4,
            out_specs=[block] * 4,
            compiler_params=pltpu.CompilerParams(vmem_limit_bytes=VMEM),
        )(*results)

    placed = (P(("rep", "seq", "head"), None),) * 4
    return jax.shard_map(
        shards, mesh=mesh, in_specs=placed, out_specs=placed, check_vma=False
    )
```

```python
import functools

import jax
import jax.numpy as jnp
from jax import lax
from jax.experimental import pallas as pl
from jax.experimental.pallas import tpu as pltpu
from jax.sharding import PartitionSpec as P

DH = 128
SPLIT = 1
CORE_LAG = 1
CHIP_LAG = 2
TOK_LAG = 3
GROUP = 8
STEPS = 2
VMEM = 62 * 1024 * 1024

F32 = jnp.float32
BF16 = jnp.bfloat16
MESH = pl.DeviceIdType.MESH


def dot(a, b, ca, cb):
    return lax.dot_general(a, b, (((ca,), (cb,)), ((), ())), preferred_element_type=F32)


def kernel(
    n_s, n_h, heads, factor, xdt, zdt,
    q_hbm, k_hbm, v_hbm, g_hbm,
    att_hbm, dq_hbm, dk_hbm, dv_hbm,
    q_ref, k_ref, v_ref, g_ref, att_ref, dq_ref, dk_ref, dv_ref,
    own, pair, s_all, t_all, f_send, f_recv, b_send, b_recv,
    up_send, up_recv, dn_send, dn_recv,
    in_sem, out_sem, c_ss, c_rs, f_ss, f_rs, b_ss, b_rs, up_ss, up_rs, dn_ss, dn_rs,
):
    s = lax.axis_index("seq")
    h = lax.axis_index("head")
    n_p = n_s // 2
    p, c = s // 2, lax.rem(s, 2)
    units = heads * SPLIT
    rows = DH // SPLIT
    toks = q_ref.shape[0]
    groups = heads // GROUP

    def fetch(g):
        at = pl.ds(pl.multiple_of(g * GROUP * DH, GROUP * DH), GROUP * DH)
        return [
            pltpu.make_async_copy(src.at[:, at], dst.at[:, at], in_sem.at[n, g])
            for n, (src, dst) in enumerate(
                ((k_hbm, k_ref), (v_hbm, v_ref), (q_hbm, q_ref), (g_hbm, g_ref))
            )
        ]

    def put(g):
        at = pl.ds(pl.multiple_of(g * GROUP * DH, GROUP * DH), GROUP * DH)
        return [
            pltpu.make_async_copy(src.at[:, at], dst.at[:, at], out_sem.at[n, g])
            for n, (src, dst) in enumerate(
                ((att_ref, att_hbm), (dq_ref, dq_hbm), (dk_ref, dk_hbm), (dv_ref, dv_hbm))
            )
        ]

    for g in range(groups):
        for copy in fetch(g):
            copy.start()

    def remote(src, dst, ss, rs, i, to):
        return pltpu.make_async_remote_copy(
            src_ref=src, dst_ref=dst, send_sem=ss.at[i], recv_sem=rs.at[i],
            device_id=to, device_id_type=MESH,
        )

    other = 2 * p + (1 - c)
    s_up, s_dn = lax.rem(s + 2, n_s), lax.rem(s + n_s - 2, n_s)
    h_up, h_dn = lax.rem(h + 1, n_h), lax.rem(h + n_h - 1, n_h)

    def swap(i):
        return remote(own.at[i], pair.at[i], c_ss, c_rs, i, {"seq": other})

    def fwd(i):
        return remote(f_send.at[i], f_recv.at[i], f_ss, f_rs, i, {"seq": s_up})

    def bwd(i):
        return remote(b_send.at[i], b_recv.at[i], b_ss, b_rs, i, {"seq": s_dn})

    def up(i, n):
        return remote(
            up_send.at[i, pl.ds(0, n)], up_recv.at[i, pl.ds(0, n)], up_ss, up_rs, i, {"head": h_up}
        )

    def down(i, n):
        return remote(
            dn_send.at[i, pl.ds(0, n)], dn_recv.at[i, pl.ds(0, n)], dn_ss, dn_rs, i, {"head": h_dn}
        )

    p_first, p_last = p == 0, p == n_p - 1
    s_first, s_last = s == 0, s == n_s - 1
    h_first, h_last = h == 0, h == n_h - 1
    no = jnp.logical_not

    barrier = pltpu.get_barrier_semaphore()

    def greet(**to):
        pl.semaphore_signal(barrier, inc=1, device_id=to, device_id_type=MESH)

    greet(seq=other)
    pl.when(no(p_first))(lambda: greet(seq=s_dn))
    pl.when(no(p_last))(lambda: greet(seq=s_up))
    pl.when(no(h_first))(lambda: greet(head=h_dn))
    pl.when(no(h_last))(lambda: greet(head=h_up))

    @pl.when(p_first)
    def _():
        f_recv[...] = jnp.zeros_like(f_recv)

    @pl.when(p_last)
    def _():
        b_recv[...] = jnp.zeros_like(b_recv)

    @pl.when(h_first)
    def _():
        up_recv[:, 0] = jnp.zeros_like(up_recv[:, 0])

    @pl.when(h_last)
    def _():
        dn_recv[:, 0] = jnp.zeros_like(dn_recv[:, 0])

    @pl.when(jnp.logical_or(h_first, s_last))
    def _():
        up_recv[:, 1] = jnp.zeros_like(up_recv[:, 1])

    @pl.when(jnp.logical_or(h_last, s_first))
    def _():
        dn_recv[:, 1] = jnp.zeros_like(dn_recv[:, 1])

    def cols(j):
        return pl.ds(pl.multiple_of(j * DH, DH), DH)

    def states(j):
        at = cols(j)
        kv = dot(k_ref[:, at], v_ref[:, at], 0, 0)
        gs = dot(q_ref[:, at], g_ref[:, at], 0, 0)
        for r in range(SPLIT):
            own[j * SPLIT + r, 0] = kv[r * rows:(r + 1) * rows]
            own[j * SPLIT + r, 1] = gs[r * rows:(r + 1) * rows]

    row = lax.broadcasted_iota(jnp.int32, (toks, toks), 0)
    col = lax.broadcasted_iota(jnp.int32, (toks, toks), 1)
    causal = row >= col

    def apply(j):
        at = cols(j)
        q, k, v, g = q_ref[:, at], k_ref[:, at], v_ref[:, at], g_ref[:, at]
        part = pl.ds(j * SPLIT, SPLIT)
        prefix = up_recv[part, 0].astype(F32) + s_all[part] + dn_recv[part, 1].astype(F32)
        suffix = dn_recv[part, 0].astype(F32) + t_all[part] + up_recv[part, 1].astype(F32)
        prefix = (prefix * factor).astype(BF16).reshape(DH, DH)
        suffix = (suffix * factor).astype(BF16).reshape(DH, DH)
        scores = jnp.where(causal, dot(q, k, 1, 1) * factor, 0.0).astype(BF16)
        dscores = jnp.where(causal, dot(g, v, 1, 1) * factor, 0.0).astype(BF16)
        att_ref[:, at] = (dot(scores, v, 1, 0) + dot(q, prefix, 1, 0)).astype(BF16)
        dq_ref[:, at] = (dot(dscores, k, 1, 0) + dot(g, prefix, 1, 1)).astype(BF16)
        dk_ref[:, at] = (dot(dscores, q, 0, 0) + dot(v, suffix, 1, 1)).astype(BF16)
        dv_ref[:, at] = (dot(scores, g, 0, 0) + dot(k, suffix, 1, 0)).astype(BF16)

    for copy in fetch(0):
        copy.wait()
    for j in range(GROUP):
        states(j)
    pl.semaphore_wait(
        barrier,
        5 - p_first.astype(jnp.int32) - p_last.astype(jnp.int32)
        - h_first.astype(jnp.int32) - h_last.astype(jnp.int32),
    )
    for r in range(GROUP * SPLIT):
        swap(r).start()

    off_z = CORE_LAG + CHIP_LAG * (n_p - 1)
    off_e = off_z + TOK_LAG * (n_h - 1)

    def valid(i, *more):
        ok = jnp.logical_and(i >= 0, i < units)
        for cond in more:
            ok = jnp.logical_and(ok, cond)
        return ok

    def drain(i):
        swap(i).wait_send()
        pl.when(no(p_last))(lambda: fwd(i).wait_send())
        pl.when(no(p_first))(lambda: bwd(i).wait_send())
        pl.when(jnp.logical_and(no(h_last), no(s_last)))(lambda: up(i, 2).wait_send())
        pl.when(jnp.logical_and(no(h_last), s_last))(lambda: up(i, 1).wait_send())
        pl.when(jnp.logical_and(no(h_first), no(s_first)))(lambda: down(i, 2).wait_send())
        pl.when(jnp.logical_and(no(h_first), s_first))(lambda: down(i, 1).wait_send())

    def slot(t, carry):
        w = t - CORE_LAG

        @pl.when(valid(w))
        def _():
            swap(w).wait_recv()

        f = t - CORE_LAG - CHIP_LAG * p

        @pl.when(valid(f, no(p_first)))
        def _():
            fwd(f).wait_recv()

        @pl.when(valid(f, no(p_last)))
        def _():
            f_send[f] = (f_recv[f].astype(F32) + (own[f, 0] + pair[f, 0])).astype(xdt)
            fwd(f).start()

        b = t - CORE_LAG - CHIP_LAG * (n_p - 1 - p)

        @pl.when(valid(b, no(p_last)))
        def _():
            bwd(b).wait_recv()

        @pl.when(valid(b, no(p_first)))
        def _():
            b_send[b] = (b_recv[b].astype(F32) + (own[b, 1] + pair[b, 1])).astype(xdt)
            bwd(b).start()

        z = t - off_z

        @pl.when(valid(z))
        def _():
            s_all[z] = f_recv[z].astype(F32) + jnp.where(c == 1, pair[z, 0], 0.0)
            t_all[z] = b_recv[z].astype(F32) + jnp.where(c == 0, pair[z, 1], 0.0)

        u = z - TOK_LAG * h

        @pl.when(valid(u, no(h_first), no(s_last)))
        def _():
            up(u, 2).wait_recv()

        @pl.when(valid(u, no(h_first), s_last))
        def _():
            up(u, 1).wait_recv()

        @pl.when(valid(u, no(h_last)))
        def _():
            up_send[u, 0] = (up_recv[u, 0].astype(F32) + (s_all[u] + own[u, 0])).astype(zdt)

            @pl.when(no(s_last))
            def _():
                up_send[u, 1] = (up_recv[u, 1].astype(F32) + t_all[u]).astype(zdt)
                up(u, 2).start()

            @pl.when(s_last)
            def _():
                up(u, 1).start()

        d = z - TOK_LAG * (n_h - 1 - h)

        @pl.when(valid(d, no(h_last), no(s_first)))
        def _():
            down(d, 2).wait_recv()

        @pl.when(valid(d, no(h_last), s_first))
        def _():
            down(d, 1).wait_recv()

        @pl.when(valid(d, no(h_first)))
        def _():
            dn_send[d, 0] = (dn_recv[d, 0].astype(F32) + (t_all[d] + own[d, 1])).astype(zdt)

            @pl.when(no(s_first))
            def _():
                dn_send[d, 1] = (dn_recv[d, 1].astype(F32) + s_all[d]).astype(zdt)
                down(d, 2).start()

            @pl.when(s_first)
            def _():
                down(d, 1).start()

        j = (t + 1) // SPLIT + GROUP - 1

        @pl.when(jnp.logical_and(lax.rem(t + 1, SPLIT) == 0, j < heads))
        def _():
            @pl.when(lax.rem(j, GROUP) == 0)
            def _():
                for copy in fetch(j // GROUP):
                    copy.wait()

            states(j)
            for r in range(SPLIT):
                swap(j * SPLIT + r).start()

        e = t - off_e

        @pl.when(valid(e))
        def _():
            drain(e)

        @pl.when(valid(e, lax.rem(e + 1, SPLIT) == 0))
        def _():
            apply(e // SPLIT)

            @pl.when(lax.rem(e // SPLIT + 1, GROUP) == 0)
            def _():
                for copy in put(e // SPLIT // GROUP):
                    copy.start()

        return carry

    lax.fori_loop(0, units + off_e, slot, 0)

    for g in range(groups):
        for copy in put(g):
            copy.wait()


def store(*refs):
    for src, dst in zip(refs[:4], refs[4:]):
        dst[...] = src[...]


def solution(mesh):
    n_s, n_h = mesh.shape["seq"], mesh.shape["head"]

    def shards(queries, key_rows, value_rows, out_grad):
        toks, width = queries.shape
        heads = width // DH
        units, rows = heads * SPLIT, DH // SPLIT
        factor = float(DH * toks * n_h * n_s) ** (-0.5)
        xdt = BF16 if n_s <= 4 else F32
        zdt = BF16 if n_h <= 4 else F32
        tokens = pltpu.VMEM((toks, width), BF16)
        both = pltpu.VMEM((units, 2, rows, DH), F32)
        one = pltpu.VMEM((units, rows, DH), F32)
        chip = pltpu.VMEM((units, rows, DH), xdt)
        hop = pltpu.VMEM((units, 2, rows, DH), zdt)
        hbm = pl.BlockSpec(memory_space=pltpu.HBM)
        shape = [jax.ShapeDtypeStruct((toks, width), BF16)] * 4
        dma = pltpu.SemaphoreType.DMA
        results = pl.pallas_call(
            functools.partial(kernel, n_s, n_h, heads, factor, xdt, zdt),
            out_shape=shape,
            in_specs=[hbm] * 4,
            out_specs=[hbm] * 4,
            scratch_shapes=[tokens] * 8
            + [both] * 2 + [one] * 2 + [chip] * 4 + [hop] * 4
            + [dma((4, heads // GROUP))] * 2 + [dma((units,))] * 10,
            compiler_params=pltpu.CompilerParams(
                collective_id=0, has_side_effects=True, vmem_limit_bytes=VMEM
            ),
        )(queries, key_rows, value_rows, out_grad)

        block = pl.BlockSpec((toks // STEPS, width), lambda i: (i, 0))
        return pl.pallas_call(
            store,
            grid=(STEPS,),
            out_shape=shape,
            in_specs=[block] * 4,
            out_specs=[block] * 4,
            compiler_params=pltpu.CompilerParams(vmem_limit_bytes=VMEM),
        )(*results)

    placed = (P(("rep", "seq", "head"), None),) * 4
    return jax.shard_map(
        shards, mesh=mesh, in_specs=placed, out_specs=placed, check_vma=False
    )
```
